32 devices in a mesh: row: 8 (over y, x, core), col: 4 (over z).
Axes of the slice: x: 2, y: 2, z: 4, core: 2. Of those that a mesh axis runs over, the one named last changes fastest.
Arguments:
- features: bfloat16 [12288, 256], P(('row', 'col')), may hold values from -6 to 6
- weight: bfloat16 [256, 256], replicated, may hold values from -0.375 to 0.375
- out_bias: float32 [256], replicated, may hold values from -3 to 3
- cotangent: bfloat16 [12288, 256], P(('row', 'col')), may hold values from -6 to 6
- adj_tiles: bfloat16 [8, 4, 12, 16, 128, 128], P('row', 'col'), may hold values from -0.125 to 0.125
- tile_cols: int32 [8, 4, 12, 16], P('row', 'col'), may hold values from 0 to 23, as said below
- tile_counts: int32 [8, 4, 12], P('row', 'col'), may hold values from 1 to 16, as said below
Outputs:
- activated: bfloat16 [12288, 256], P(('row', 'col'))
- grad_features: bfloat16 [12288, 256], P(('row', 'col'))
- grad_weight: float32 [256, 256], replicated
- grad_bias: float32 [256], replicated
The draws below stay inside these ranges and needn't reach their ends.
Inputs may be any that keep to these rules, and one draw needn't show every extreme that they name: `tile_cols`: within a tile row of a block the 16 column numbers are distinct. `tile_counts`: every block has a tile row whose 16 slots are all live.
All inputs are finite; a program needn't handle non-finite values.
Results may differ from the reference program's by a relative error of at most 0.02.
Values may be sent and summed in bfloat16 or wider, within the bound.
A program may use at most 192 MiB of HBM per device.

```python
import jax
import jax.numpy as jnp
from jax import lax

F = 256
TILE = 128
K = 16
ND = 384
ROW_BLOCKS = 8
COL_BLOCKS = 4
NODES = 12288
TR = 12
TC = 24


def draw_tile_cols(key, part):
    shape_all = (ROW_BLOCKS, COL_BLOCKS, TR, TC)
    scores = jax.random.randint(key, shape_all, 0, 1 << 20) * TC + lax.broadcasted_iota(jnp.int32, shape_all, 3)
    ordering = jnp.argsort(scores, axis=3)
    return ordering[..., :K].astype(jnp.int32)


def draw_tile_counts(key, part):
    first_key, second_key, third_key = jax.random.split(key, 3)
    lowest = max(1, K // 4)
    highest = jax.random.randint(first_key, (ROW_BLOCKS, COL_BLOCKS, 1), lowest, K + 1)
    bottom = jnp.maximum(highest // 2, 1)
    raw_draw = jax.random.randint(second_key, (ROW_BLOCKS, COL_BLOCKS, TR), 0, 1 << 20)
    counted = bottom + raw_draw % (highest - bottom + 1)
    full_row = jax.random.randint(third_key, (ROW_BLOCKS, COL_BLOCKS, 1), 0, TR)
    row_iota = lax.broadcasted_iota(jnp.int32, (ROW_BLOCKS, COL_BLOCKS, TR), 2)
    return jnp.where(row_iota == full_row, K, counted).astype(jnp.int32)


def block_scale(stream_key, shape, shards, least, top_value):
    factor_of = 1.0
    for position, shards_of in shards:
        steps = jax.random.uniform(jax.random.fold_in(jax.random.fold_in(stream_key, 6), position), (shards_of,), jnp.float32, least / len(shards), top_value / len(shards))
        factor_of = factor_of * jnp.repeat(jnp.exp(steps), shape[position] // shards_of).reshape((-1,) + (1,) * (len(shape) - 1 - position))
    return factor_of


def centred(key, dims, deviation, limit, pieces=(), kind=jnp.bfloat16):
    loudness = block_scale(key, dims, pieces, -0.22, 0.18) if pieces else 1.0
    drawn = jax.random.normal(key, dims, jnp.float32) * deviation * loudness
    return jnp.minimum(jnp.maximum(drawn, -limit), limit).astype(kind)


def setup_inputs(seed: int = 0) -> dict:
    key_of = jax.random.split(jax.random.key(seed), 8)
    return {
        "features": centred(key_of[0], (NODES, F), 1.0, 6.0, ((0, 32),)),
        "weight": centred(key_of[1], (F, F), F ** -0.5, 0.375),
        "out_bias": centred(key_of[2], (F,), 0.5, 3.0, (), jnp.float32),
        "cotangent": centred(key_of[3], (NODES, F), 1.0, 6.0, ((0, 32),)),
        "adj_tiles": centred(key_of[4], (ROW_BLOCKS, COL_BLOCKS, TR, K, TILE, TILE), (K * TILE) ** -0.5, 0.125, ((0, 8), (1, 4))),
        "tile_cols": draw_tile_cols(jax.random.fold_in(key_of[7], 71), 0),
        "tile_counts": draw_tile_counts(jax.random.fold_in(key_of[7], 71), 0),
    }


def reference(features, weight, out_bias, cotangent, adj_tiles, tile_cols, tile_counts):
    feat_width = features.shape[1]
    nodes_all = features.shape[0]
    block_count = ROW_BLOCKS * COL_BLOCKS
    projected = jnp.dot(features, weight, preferred_element_type=jnp.float32).astype(jnp.bfloat16)
    proj_four = projected.reshape(ROW_BLOCKS, COL_BLOCKS, ND, feat_width)
    panels = jnp.transpose(proj_four, (1, 0, 2, 3)).reshape(COL_BLOCKS, TC, TILE, feat_width)
    slot_iota = lax.broadcasted_iota(jnp.int32, (ROW_BLOCKS, COL_BLOCKS, TR, K), 3)
    live_mask = (slot_iota < tile_counts[..., None]).astype(jnp.float32).reshape(block_count, TR, K)
    flat_tiles = adj_tiles.reshape(block_count, TR, K, TILE, TILE)
    flat_cols = tile_cols.reshape(block_count, TR, K)
    block_ids = jnp.arange(block_count, dtype=jnp.int32)

    def forward_block(inputs):
        block_vals, cols_block, live_block, ident = inputs
        col_index = (ident % COL_BLOCKS).astype(jnp.int32)
        gathered = lax.dynamic_index_in_dim(panels, col_index, 0, keepdims=False)
        picked = gathered[cols_block].astype(jnp.float32)
        masked = block_vals.astype(jnp.float32) * live_block[:, :, None, None]
        return jnp.einsum('tkab,tkbf->taf', masked, picked).astype(jnp.bfloat16)

    partial_value = lax.map(forward_block, (flat_tiles, flat_cols, live_mask, block_ids))
    partial_value = lax.optimization_barrier(partial_value).astype(jnp.float32)
    summed = partial_value.reshape(ROW_BLOCKS, COL_BLOCKS, TR * TILE, feat_width).sum(axis=1)
    preact = summed.reshape(nodes_all, feat_width) + out_bias
    sigmoid_val = jax.nn.sigmoid(preact)
    activated = (preact * sigmoid_val).astype(jnp.bfloat16)
    grad_preact = (cotangent.astype(jnp.float32) * sigmoid_val * (1.0 + preact * (1.0 - sigmoid_val))).astype(jnp.bfloat16)
    grad_rows = grad_preact.reshape(ROW_BLOCKS, TR, TILE, feat_width)

    def backward_block(inputs):
        block_vals, cols_block, live_block, ident = inputs
        row_index = (ident // COL_BLOCKS).astype(jnp.int32)
        rows_here = lax.dynamic_index_in_dim(grad_rows, row_index, 0, keepdims=False).astype(jnp.float32)
        masked = block_vals.astype(jnp.float32) * live_block[:, :, None, None]
        products = jnp.einsum('tkab,taf->tkbf', masked, rows_here)
        running = jnp.zeros((TC, TILE, feat_width), jnp.float32).at[cols_block].add(products)
        return running.astype(jnp.bfloat16)

    back = lax.map(backward_block, (flat_tiles, flat_cols, live_mask, block_ids))
    back = lax.optimization_barrier(back).astype(jnp.float32)
    column_total = back.reshape(ROW_BLOCKS, COL_BLOCKS, TC * TILE, feat_width).sum(axis=0)
    column_total = column_total.reshape(COL_BLOCKS, ROW_BLOCKS, ND, feat_width)
    grad_projected = jnp.transpose(column_total, (1, 0, 2, 3)).reshape(nodes_all, feat_width).astype(jnp.bfloat16)
    grad_features = jnp.dot(grad_projected, weight.T, preferred_element_type=jnp.float32).astype(jnp.bfloat16)
    scale_factor = nodes_all ** -0.5
    grad_weight = jnp.dot(features.T, grad_projected, preferred_element_type=jnp.float32) * scale_factor
    grad_bias = jnp.sum(grad_preact.astype(jnp.float32), axis=0) * scale_factor
    return (activated, grad_features, grad_weight, grad_bias)
```

```python
import functools

import jax
import jax.numpy as jnp
from jax import lax
from jax.experimental import pallas as pl
from jax.experimental.pallas import tpu as pltpu
from jax.sharding import PartitionSpec as P

MESH = pl.DeviceIdType.MESH
BF = jnp.bfloat16
F32 = jnp.float32


def aligned(index, size):
    return pl.ds(pl.multiple_of(index * size, size), size)


def kernel(
    rows, cols, nd, slots, tile, buffers, scale,
    slot_ref, feat_ref, weight_ref, bias_ref, cot_ref, adj_ref,
    act_ref, gfeat_ref, gweight_ref, gbias_ref,
    dense, panel, part, inbox, total, grads, grad_t, acc, back, sib_in, row_in,
    feat_t, w_out, w_in, w_col, w_all,
    load_sem, ag_send, ag_recv, fw_send, fw_recv, up_send, up_recv, dn_send, dn_recv,
    gu_send, gd_send, g_recv, sb_send, sb_recv, rs_send, rs_recv,
    w1_send, w1_recv, w2_send, w2_recv, w3_send, w3_recv,
    *tiles,
):
    r, z = lax.axis_index("row"), lax.axis_index("col")
    width = feat_ref.shape[1]
    chips = rows // 2
    chip, core = r // 2, r % 2
    sibling = 2 * chip + 1 - core
    per = nd // tile
    group = per * slots
    col_tiles = rows * per
    piece = width // rows

    def remote(src, dst, send, recv, row, col):
        return pltpu.make_async_remote_copy(
            src_ref=src, dst_ref=dst, send_sem=send, recv_sem=recv,
            device_id=(row, col), device_id_type=MESH,
        )

    def load(g):
        return pltpu.make_async_copy(
            adj_ref.at[pl.ds(g * group, group)],
            tiles[g % buffers].at[pl.ds(0, group)],
            load_sem.at[g % buffers],
        )

    for g in range(min(buffers, cols)):
        load(g).start()

    barrier = pltpu.get_barrier_semaphore()
    for o in range(1, rows):
        pl.semaphore_signal(barrier, inc=1, device_id=((r + o) % rows, z), device_id_type=MESH)
    for o in range(1, cols):
        pl.semaphore_signal(barrier, inc=1, device_id=(r, (z + o) % cols), device_id_type=MESH)
    projected = jnp.dot(feat_ref[...], weight_ref[...], preferred_element_type=F32).astype(BF)
    mine = aligned(r, nd)
    panel[mine, :] = projected
    pl.semaphore_wait(barrier, rows + cols - 2)

    def ag(o, to):
        return remote(panel.at[mine], panel.at[mine], ag_send.at[o], ag_recv.at[o], to, z)

    def forward(o):
        src = aligned(2 * ((chip + chips - o) % chips) + core, nd)
        return remote(panel.at[src], panel.at[src], fw_send.at[o], fw_recv.at[o], sibling, z)

    def forward_in(o):
        src = aligned(2 * ((chip + chips - o) % chips) + 1 - core, nd)
        return remote(panel.at[src], panel.at[src], fw_send.at[o], fw_recv.at[o], sibling, z)

    for o in range(1, chips):
        ag(o, 2 * ((chip + o) % chips) + core).start()
    forward(0).start()

    feat_t[...] = feat_ref[...].astype(F32).T.astype(BF)
    for b in range(buffers):
        tiles[b][group] = jnp.zeros((tile, tile), BF)
    for g in range(cols):
        buf = tiles[g % buffers]
        load(g).wait()

        def spread(t, carry, g=g, buf=buf):
            at = aligned(g * per + t, tile)
            for j in range(col_tiles):
                dense[at, pl.ds(j * tile, tile)] = buf[slot_ref[g * per + t, j]]
            return carry

        lax.fori_loop(0, per, spread, 0)
        if g + buffers < cols:
            load(g + buffers).start()

    for o in range(1, chips):
        src = aligned(2 * ((chip + chips - o) % chips) + core, nd)
        remote(panel.at[src], panel.at[src], ag_send.at[o], ag_recv.at[o], r, z).wait_recv()
        forward(o).start()
    for o in range(chips):
        forward_in(o).wait_recv()

    def up_copy(d):
        return remote(part.at[aligned(d, nd)], inbox.at[aligned(d + 1, nd)], up_send.at[d], up_recv.at[d], r, z + 1)

    def up_wait(d):
        remote(part.at[aligned(d, nd)], inbox.at[aligned(d + 1, nd)], up_send.at[d], up_recv.at[d], r, z).wait_recv()

    def down_copy(d):
        return remote(part.at[aligned(d, nd)], inbox.at[aligned(d, nd)], dn_send.at[d], dn_recv.at[d], r, z - 1)

    def down_wait(d):
        remote(part.at[aligned(d, nd)], inbox.at[aligned(d, nd)], dn_send.at[d], dn_recv.at[d], r, z).wait_recv()

    low = (z < cols // 2).astype(jnp.int32)

    def produce(s, carry):
        d = low * (cols - 1 - s) + (1 - low) * s
        at = aligned(d, nd)
        part[at, :] = jnp.dot(dense[at, :], panel[...], preferred_element_type=F32).astype(BF)

        @pl.when((z == 0) & (d > z))
        def _():
            up_copy(d).start()

        @pl.when((z == cols - 1) & (d < z))
        def _():
            down_copy(d).start()

        return carry

    lax.fori_loop(0, cols, produce, 0)

    for s in range(cols):
        d = cols - 1 - s

        @pl.when((d > z) & (z > 0))
        def _(d=d):
            at = pl.ds(d * nd, nd)
            up_wait(d)
            part[at, :] = (part[at, :].astype(F32) + inbox[pl.ds((d + 1) * nd, nd), :].astype(F32)).astype(BF)
            up_copy(d).start()

        @pl.when((s < z) & (z < cols - 1))
        def _(d=s):
            at = pl.ds(d * nd, nd)
            down_wait(d)
            part[at, :] = (part[at, :].astype(F32) + inbox[at, :].astype(F32)).astype(BF)
            down_copy(d).start()

    here = aligned(z, nd)
    total[...] = part[here, :].astype(F32) + bias_ref[...]

    @pl.when(z > 0)
    def _():
        up_wait(z)
        total[...] += inbox[aligned(z + 1, nd), :].astype(F32)

    @pl.when(z < cols - 1)
    def _():
        down_wait(z)
        total[...] += inbox[here, :].astype(F32)

    preact = total[...]
    sig = jax.nn.sigmoid(preact)
    grads[here, :] = (cot_ref[...].astype(F32) * sig * (1.0 + preact * (1.0 - sig))).astype(BF)

    def g_copy(b, send, to):
        return remote(grads.at[aligned(b, nd)], grads.at[aligned(b, nd)], send.at[b], g_recv.at[b], r, to)

    @pl.when(z < cols - 1)
    def _():
        g_copy(z, gu_send, z + 1).start()

    @pl.when(z > 0)
    def _():
        g_copy(z, gd_send, z - 1).start()

    act_ref[...] = (preact * sig).astype(BF)

    span = 2 * nd

    def backward(b, first):
        grad_t[...] = grads[aligned(b, nd), :].astype(F32).T.astype(BF)
        at = aligned(b, nd)

        def step(i, carry):
            lanes = aligned(i, span)
            product = jnp.dot(grad_t[...], dense[at, lanes], preferred_element_type=F32)
            if first:
                acc[:, lanes] = product
            else:
                acc[:, lanes] += product
            return carry

        lax.fori_loop(0, rows // 2, step, 0)

    backward(z, True)
    for o in range(1, cols):

        @pl.when(z - o >= 0)
        def _(o=o):
            g_copy(z - o, gu_send, z).wait_recv()

            @pl.when(z < cols - 1)
            def _():
                g_copy(z - o, gu_send, z + 1).start()

        @pl.when(z + o < cols)
        def _(o=o):
            g_copy(z + o, gd_send, z).wait_recv()

            @pl.when(z > 0)
            def _():
                g_copy(z + o, gd_send, z - 1).start()

        @pl.when(z - o >= 0)
        def _(o=o):
            backward(z - o, False)

        @pl.when(z + o < cols)
        def _(o=o):
            backward(z + o, False)

    def sib_copy(m):
        return remote(back.at[2 * m + 1 - core], sib_in.at[m], sb_send.at[m], sb_recv.at[m], sibling, z)

    def lanes_of(dest):
        return aligned(dest, nd)

    for o in range(chips):
        m = (chip + 1 + o) % chips
        dest = 2 * m + 1 - core
        back[dest] = acc[:, lanes_of(dest)].astype(BF)
        sib_copy(m).start()

    def row_copy(o):
        m = (chip + o) % chips
        return remote(back.at[2 * m + core], row_in.at[o], rs_send.at[o], rs_recv.at[o], 2 * m + core, z)

    for o in range(1, chips):
        m = (chip + o) % chips
        dest = 2 * m + core
        sib_copy(m).wait_recv()
        back[dest] = (acc[:, lanes_of(dest)] + sib_in[m].astype(F32)).astype(BF)
        row_copy(o).start()

    bias_row = jnp.sum(grads[...].astype(F32), axis=0, keepdims=True)
    high = bias_row.astype(BF)
    rest = (bias_row - high.astype(F32)).astype(BF).astype(F32)
    line = lax.broadcasted_iota(jnp.int32, (16, width), 0)
    bias_rows = jnp.where(line == 0, high.astype(F32), jnp.where(line == 1, rest, 0.0)).astype(BF)

    sib_copy(chip).wait_recv()
    summed = acc[:, lanes_of(r)] + sib_in[chip].astype(F32)
    for o in range(1, chips):
        row_copy(o).wait_recv()
        summed = summed + row_in[o].astype(F32)
    gp = summed.T.astype(BF)

    w_part = jnp.dot(feat_t[...], gp, preferred_element_type=F32).astype(BF)
    for i in range(rows):
        w_out[i, pl.ds(0, piece), :] = w_part[i * piece:(i + 1) * piece]
        w_out[i, pl.ds(piece, 16), :] = bias_rows

    def w1(o):
        to = (r + o) % rows
        return remote(w_out.at[to], w_in.at[r], w1_send.at[o], w1_recv.at[o], to, z)

    def w1_wait(o):
        src = (r + rows - o) % rows
        remote(w_out.at[src], w_in.at[src], w1_send.at[o], w1_recv.at[o], src, z).wait_recv()

    for o in range(1, rows):
        w1(o).start()
    w_in[r] = w_out[r]
    gfeat_ref[...] = lax.dot_general(
        gp, weight_ref[...], (((1,), (1,)), ((), ())), preferred_element_type=F32
    ).astype(BF)
    for o in range(1, rows):
        w1_wait(o)
    part_sum = w_in[0].astype(F32)
    for i in range(1, rows):
        part_sum = part_sum + w_in[i].astype(F32)
    w_col[z] = part_sum[:piece].astype(BF)

    def w2(o):
        to = (z + o) % cols
        return remote(w_col.at[z], w_col.at[z], w2_send.at[o], w2_recv.at[o], r, to)

    def w2_wait(o):
        src = (z + cols - o) % cols
        remote(w_col.at[src], w_col.at[src], w2_send.at[o], w2_recv.at[o], r, src).wait_recv()

    for o in range(1, cols):
        w2(o).start()
    gbias_ref[...] = (part_sum[piece:piece + 1] + part_sum[piece + 1:piece + 2]) * scale
    for o in range(1, cols):
        w2_wait(o)
    col_sum = w_col[0].astype(F32)
    for i in range(1, cols):
        col_sum = col_sum + w_col[i].astype(F32)
    w_all[r] = col_sum.astype(BF)

    def w3(o):
        to = (r + o) % rows
        return remote(w_all.at[r], w_all.at[r], w3_send.at[o], w3_recv.at[o], to, z)

    def w3_wait(o):
        src = (r + rows - o) % rows
        remote(w_all.at[src], w_all.at[src], w3_send.at[o], w3_recv.at[o], src, z).wait_recv()

    for o in range(1, rows):
        w3(o).start()

    for o in range(1, chips):
        ag(o, 2 * ((chip + o) % chips) + core).wait_send()
        row_copy(o).wait_send()
    for o in range(chips):
        forward(o).wait_send()
        sib_copy((chip + 1 + o) % chips).wait_send()
    for d in range(cols):

        @pl.when(d > z)
        def _(d=d):
            up_copy(d).wait_send()

        @pl.when(d < z)
        def _(d=d):
            down_copy(d).wait_send()

        @pl.when((d <= z) & (z < cols - 1))
        def _(d=d):
            g_copy(d, gu_send, z + 1).wait_send()

        @pl.when((d >= z) & (z > 0))
        def _(d=d):
            g_copy(d, gd_send, z - 1).wait_send()

    for o in range(1, cols):
        w2(o).wait_send()
    for o in range(1, rows):
        w1(o).wait_send()
        w3_wait(o)
    for i in range(rows):
        gweight_ref[pl.ds(i * piece, piece), :] = w_all[i].astype(F32) * scale
    for o in range(1, rows):
        w3(o).wait_send()


def shards(features, weight, out_bias, cotangent, adj_tiles, tile_cols, tile_counts):
    nd, width = features.shape
    tile = adj_tiles.shape[-1]
    slots = adj_tiles.shape[3]
    tile_rows = adj_tiles.shape[2]
    rows, cols = lax.axis_size("row"), lax.axis_size("col")
    per = nd // tile
    col_tiles = rows * per
    chips = rows // 2
    blocks = adj_tiles.reshape(tile_rows * slots, tile, tile)
    columns = tile_cols.reshape(tile_rows, slots)
    counts = tile_counts.reshape(tile_rows)
    k = lax.broadcasted_iota(jnp.int32, (tile_rows, slots, col_tiles), 1)
    j = lax.broadcasted_iota(jnp.int32, (tile_rows, slots, col_tiles), 2)
    t = lax.broadcasted_iota(jnp.int32, (tile_rows, slots, col_tiles), 0)
    found = (columns[:, :, None] == j) & (k < counts[:, None, None])
    slot = jnp.min(jnp.where(found, (t % per) * slots + k, per * slots), axis=1)
    big = tile_rows * col_tiles * tile * tile * 2 > 16 * 2**20
    buffers = 2 if big else min(4, cols)
    piece = width // rows
    dma = lambda n: pltpu.SemaphoreType.DMA((n,))
    vmem = pl.BlockSpec(memory_space=pltpu.VMEM)
    scale = (nd * rows * cols) ** (-0.5)
    act, gfeat, gweight, gbias = pl.pallas_call(
        functools.partial(kernel, rows, cols, nd, slots, tile, buffers, scale),
        out_shape=(
            jax.ShapeDtypeStruct((nd, width), BF),
            jax.ShapeDtypeStruct((nd, width), BF),
            jax.ShapeDtypeStruct((width, width), F32),
            jax.ShapeDtypeStruct((1, width), F32),
        ),
        in_specs=[pl.BlockSpec(memory_space=pltpu.SMEM)] + [vmem] * 4 + [pl.BlockSpec(memory_space=pl.ANY)],
        out_specs=(vmem,) * 4,
        scratch_shapes=[
            pltpu.VMEM((tile_rows * tile, col_tiles * tile), BF),
            pltpu.VMEM((rows * nd, width), BF),
            pltpu.VMEM((cols * nd, width), BF),
            pltpu.VMEM(((cols + 1) * nd, width), BF),
            pltpu.VMEM((nd, width), F32),
            pltpu.VMEM((cols * nd, width), BF),
            pltpu.VMEM((width, nd), BF),
            pltpu.VMEM((width, rows * nd), F32),
            pltpu.VMEM((rows, width, nd), BF),
            pltpu.VMEM((chips, width, nd), BF),
            pltpu.VMEM((chips, width, nd), BF),
            pltpu.VMEM((width, nd), BF),
            pltpu.VMEM((rows, piece + 16, width), BF),
            pltpu.VMEM((rows, piece + 16, width), BF),
            pltpu.VMEM((cols, piece, width), BF),
            pltpu.VMEM((rows, piece, width), BF),
            dma(buffers),
            dma(chips), dma(chips), dma(chips), dma(chips),
            dma(cols), dma(cols), dma(cols), dma(cols),
            dma(cols), dma(cols), dma(cols),
            dma(chips), dma(chips), dma(chips), dma(chips),
            dma(rows), dma(rows), dma(cols), dma(cols), dma(rows), dma(rows),
        ] + [pltpu.VMEM((per * slots + 1, tile, tile), BF)] * buffers,
        compiler_params=pltpu.CompilerParams(
            collective_id=0, has_side_effects=True, vmem_limit_bytes=(63 if big else 48) * 2**20
        ),
    )(slot, features, weight, out_bias.reshape(1, width), cotangent, blocks)
    return act, gfeat, gweight, gbias.reshape(width)


def solution(mesh):
    in_specs = (
        P(("row", "col"), None),
        P(),
        P(),
        P(("row", "col"), None),
        P("row", "col", None, None, None, None),
        P("row", "col", None, None),
        P("row", "col", None),
    )
    out_specs = (P(("row", "col"), None), P(("row", "col"), None), P(), P())
    return jax.shard_map(shards, mesh=mesh, in_specs=in_specs, out_specs=out_specs, check_vma=False)
```

```python
import functools

import jax
import jax.numpy as jnp
from jax import lax
from jax.experimental import pallas as pl
from jax.experimental.pallas import tpu as pltpu
from jax.sharding import PartitionSpec as P

MESH = pl.DeviceIdType.MESH
BF = jnp.bfloat16
F32 = jnp.float32


def aligned(index, size):
    return pl.ds(pl.multiple_of(index * size, size), size)


def kernel(
    rows, cols, nd, slots, tile, buffers, scale,
    slot_ref, feat_ref, weight_ref, bias_ref, cot_ref, adj_ref,
    act_ref, gfeat_ref, gweight_ref, gbias_ref,
    dense, panel, part, inbox, total, grads, grad_t, acc, back, sib_in, row_in,
    feat_t, w_out, w_in, w_col, w_all,
    load_sem, ag_send, ag_recv, fw_send, fw_recv, up_send, up_recv, dn_send, dn_recv,
    gu_send, gd_send, g_recv, sb_send, sb_recv, rs_send, rs_recv,
    w1_send, w1_recv, w2_send, w2_recv, w3_send, w3_recv,
    *tiles,
):
    r, z = lax.axis_index("row"), lax.axis_index("col")
    width = feat_ref.shape[1]
    chips = rows // 2
    chip, core = r // 2, r % 2
    sibling = 2 * chip + 1 - core
    per = nd // tile
    group = per * slots
    col_tiles = rows * per
    piece = width // rows

    def remote(src, dst, send, recv, row, col):
        return pltpu.make_async_remote_copy(
            src_ref=src, dst_ref=dst, send_sem=send, recv_sem=recv,
            device_id=(row, col), device_id_type=MESH,
        )

    def load(g):
        return pltpu.make_async_copy(
            adj_ref.at[pl.ds(g * group, group)],
            tiles[g % buffers].at[pl.ds(0, group)],
            load_sem.at[g % buffers],
        )

    for g in range(min(buffers, cols)):
        load(g).start()

    barrier = pltpu.get_barrier_semaphore()
    for o in range(1, rows):
        pl.semaphore_signal(barrier, inc=1, device_id=((r + o) % rows, z), device_id_type=MESH)
    for o in range(1, cols):
        pl.semaphore_signal(barrier, inc=1, device_id=(r, (z + o) % cols), device_id_type=MESH)
    projected = jnp.dot(feat_ref[...], weight_ref[...], preferred_element_type=F32).astype(BF)
    mine = aligned(r, nd)
    panel[mine, :] = projected
    pl.semaphore_wait(barrier, rows + cols - 2)

    def ag(o, to):
        return remote(panel.at[mine], panel.at[mine], ag_send.at[o], ag_recv.at[o], to, z)

    def forward(o):
        src = aligned(2 * ((chip + chips - o) % chips) + core, nd)
        return remote(panel.at[src], panel.at[src], fw_send.at[o], fw_recv.at[o], sibling, z)

    def forward_in(o):
        src = aligned(2 * ((chip + chips - o) % chips) + 1 - core, nd)
        return remote(panel.at[src], panel.at[src], fw_send.at[o], fw_recv.at[o], sibling, z)

    for o in range(1, chips):
        ag(o, 2 * ((chip + o) % chips) + core).start()
    forward(0).start()

    feat_t[...] = feat_ref[...].astype(F32).T.astype(BF)
    for b in range(buffers):
        tiles[b][group] = jnp.zeros((tile, tile), BF)
    for g in range(cols):
        buf = tiles[g % buffers]
        load(g).wait()

        def spread(t, carry, g=g, buf=buf):
            at = aligned(g * per + t, tile)
            for j in range(col_tiles):
                dense[at, pl.ds(j * tile, tile)] = buf[slot_ref[g * per + t, j]]
            return carry

        lax.fori_loop(0, per, spread, 0)
        if g + buffers < cols:
            load(g + buffers).start()

    for o in range(1, chips):
        src = aligned(2 * ((chip + chips - o) % chips) + core, nd)
        remote(panel.at[src], panel.at[src], ag_send.at[o], ag_recv.at[o], r, z).wait_recv()
        forward(o).start()
    for o in range(chips):
        forward_in(o).wait_recv()

    def up_copy(d):
        return remote(part.at[aligned(d, nd)], inbox.at[aligned(d + 1, nd)], up_send.at[d], up_recv.at[d], r, z + 1)

    def up_wait(d):
        remote(part.at[aligned(d, nd)], inbox.at[aligned(d + 1, nd)], up_send.at[d], up_recv.at[d], r, z).wait_recv()

    def down_copy(d):
        return remote(part.at[aligned(d, nd)], inbox.at[aligned(d, nd)], dn_send.at[d], dn_recv.at[d], r, z - 1)

    def down_wait(d):
        remote(part.at[aligned(d, nd)], inbox.at[aligned(d, nd)], dn_send.at[d], dn_recv.at[d], r, z).wait_recv()

    low = (z < cols // 2).astype(jnp.int32)

    def produce(s, carry):
        d = low * (cols - 1 - s) + (1 - low) * s
        at = aligned(d, nd)
        part[at, :] = jnp.dot(dense[at, :], panel[...], preferred_element_type=F32).astype(BF)

        @pl.when((z == 0) & (d > z))
        def _():
            @pl.when(s > 0)
            def _():
                up_copy(d + 1).wait_send()

            up_copy(d).start()

        @pl.when((z == cols - 1) & (d < z))
        def _():
            @pl.when(s > 0)
            def _():
                down_copy(d - 1).wait_send()

            down_copy(d).start()

        return carry

    lax.fori_loop(0, cols, produce, 0)

    for s in range(cols):
        d = cols - 1 - s

        @pl.when((d > z) & (z > 0))
        def _(d=d):
            at = pl.ds(d * nd, nd)
            up_wait(d)
            part[at, :] = (part[at, :].astype(F32) + inbox[pl.ds((d + 1) * nd, nd), :].astype(F32)).astype(BF)
            up_copy(d).start()

        @pl.when((s < z) & (z < cols - 1))
        def _(d=s):
            at = pl.ds(d * nd, nd)
            down_wait(d)
            part[at, :] = (part[at, :].astype(F32) + inbox[at, :].astype(F32)).astype(BF)
            down_copy(d).start()

    here = aligned(z, nd)
    total[...] = part[here, :].astype(F32) + bias_ref[...]

    @pl.when(z > 0)
    def _():
        up_wait(z)
        total[...] += inbox[aligned(z + 1, nd), :].astype(F32)

    @pl.when(z < cols - 1)
    def _():
        down_wait(z)
        total[...] += inbox[here, :].astype(F32)

    preact = total[...]
    sig = jax.nn.sigmoid(preact)
    grads[here, :] = (cot_ref[...].astype(F32) * sig * (1.0 + preact * (1.0 - sig))).astype(BF)

    def g_copy(b, send, to):
        return remote(grads.at[aligned(b, nd)], grads.at[aligned(b, nd)], send.at[b], g_recv.at[b], r, to)

    @pl.when(z < cols - 1)
    def _():
        g_copy(z, gu_send, z + 1).start()

    @pl.when(z > 0)
    def _():
        g_copy(z, gd_send, z - 1).start()

    act_ref[...] = (preact * sig).astype(BF)

    span = 2 * nd

    def backward(b, first):
        grad_t[...] = grads[aligned(b, nd), :].astype(F32).T.astype(BF)
        at = aligned(b, nd)

        def step(i, carry):
            lanes = aligned(i, span)
            product = jnp.dot(grad_t[...], dense[at, lanes], preferred_element_type=F32)
            if first:
                acc[:, lanes] = product
            else:
                acc[:, lanes] += product
            return carry

        lax.fori_loop(0, rows // 2, step, 0)

    backward(z, True)
    for o in range(1, cols):

        @pl.when(z - o >= 0)
        def _(o=o):
            g_copy(z - o, gu_send, z).wait_recv()

            @pl.when(z < cols - 1)
            def _():
                g_copy(z - o, gu_send, z + 1).start()

        @pl.when(z + o < cols)
        def _(o=o):
            g_copy(z + o, gd_send, z).wait_recv()

            @pl.when(z > 0)
            def _():
                g_copy(z + o, gd_send, z - 1).start()

        @pl.when(z - o >= 0)
        def _(o=o):
            backward(z - o, False)

        @pl.when(z + o < cols)
        def _(o=o):
            backward(z + o, False)

    def sib_copy(m):
        return remote(back.at[2 * m + 1 - core], sib_in.at[m], sb_send.at[m], sb_recv.at[m], sibling, z)

    def lanes_of(dest):
        return aligned(dest, nd)

    for o in range(chips):
        m = (chip + 1 + o) % chips
        dest = 2 * m + 1 - core
        back[dest] = acc[:, lanes_of(dest)].astype(BF)
        sib_copy(m).start()

    def row_copy(o):
        m = (chip + o) % chips
        return remote(back.at[2 * m + core], row_in.at[o], rs_send.at[o], rs_recv.at[o], 2 * m + core, z)

    for o in range(1, chips):
        m = (chip + o) % chips
        dest = 2 * m + core
        sib_copy(m).wait_recv()
        back[dest] = (acc[:, lanes_of(dest)] + sib_in[m].astype(F32)).astype(BF)
        row_copy(o).start()

    bias_row = jnp.sum(grads[...].astype(F32), axis=0, keepdims=True)
    high = bias_row.astype(BF)
    rest = (bias_row - high.astype(F32)).astype(BF).astype(F32)
    line = lax.broadcasted_iota(jnp.int32, (16, width), 0)
    bias_rows = jnp.where(line == 0, high.astype(F32), jnp.where(line == 1, rest, 0.0)).astype(BF)

    sib_copy(chip).wait_recv()
    summed = acc[:, lanes_of(r)] + sib_in[chip].astype(F32)
    for o in range(1, chips):
        row_copy(o).wait_recv()
        summed = summed + row_in[o].astype(F32)
    gp = summed.T.astype(BF)

    w_part = jnp.dot(feat_t[...], gp, preferred_element_type=F32).astype(BF)
    for i in range(rows):
        w_out[i, pl.ds(0, piece), :] = w_part[i * piece:(i + 1) * piece]
        w_out[i, pl.ds(piece, 16), :] = bias_rows

    def w1(o):
        to = (r + o) % rows
        return remote(w_out.at[to], w_in.at[r], w1_send.at[o], w1_recv.at[o], to, z)

    def w1_wait(o):
        src = (r + rows - o) % rows
        remote(w_out.at[src], w_in.at[src], w1_send.at[o], w1_recv.at[o], src, z).wait_recv()

    for o in range(1, rows):
        w1(o).start()
    w_in[r] = w_out[r]
    gfeat_ref[...] = lax.dot_general(
        gp, weight_ref[...], (((1,), (1,)), ((), ())), preferred_element_type=F32
    ).astype(BF)
    for o in range(1, rows):
        w1_wait(o)
    part_sum = w_in[0].astype(F32)
    for i in range(1, rows):
        part_sum = part_sum + w_in[i].astype(F32)
    w_col[z] = part_sum[:piece].astype(BF)

    def w2(o):
        to = (z + o) % cols
        return remote(w_col.at[z], w_col.at[z], w2_send.at[o], w2_recv.at[o], r, to)

    def w2_wait(o):
        src = (z + cols - o) % cols
        remote(w_col.at[src], w_col.at[src], w2_send.at[o], w2_recv.at[o], r, src).wait_recv()

    for o in range(1, cols):
        w2(o).start()
    gbias_ref[...] = (part_sum[piece:piece + 1] + part_sum[piece + 1:piece + 2]) * scale
    for o in range(1, cols):
        w2_wait(o)
    col_sum = w_col[0].astype(F32)
    for i in range(1, cols):
        col_sum = col_sum + w_col[i].astype(F32)
    w_all[r] = col_sum.astype(BF)

    def w3(o):
        to = (r + o) % rows
        return remote(w_all.at[r], w_all.at[r], w3_send.at[o], w3_recv.at[o], to, z)

    def w3_wait(o):
        src = (r + rows - o) % rows
        remote(w_all.at[src], w_all.at[src], w3_send.at[o], w3_recv.at[o], src, z).wait_recv()

    for o in range(1, rows):
        w3(o).start()

    for o in range(1, chips):
        ag(o, 2 * ((chip + o) % chips) + core).wait_send()
        row_copy(o).wait_send()
    for o in range(chips):
        forward(o).wait_send()
        sib_copy((chip + 1 + o) % chips).wait_send()
    for d in range(cols):

        @pl.when((d > z) & ((z > 0) | (d == z + 1)))
        def _(d=d):
            up_copy(d).wait_send()

        @pl.when((d < z) & ((z < cols - 1) | (d == z - 1)))
        def _(d=d):
            down_copy(d).wait_send()

        @pl.when((d <= z) & (z < cols - 1))
        def _(d=d):
            g_copy(d, gu_send, z + 1).wait_send()

        @pl.when((d >= z) & (z > 0))
        def _(d=d):
            g_copy(d, gd_send, z - 1).wait_send()

    for o in range(1, cols):
        w2(o).wait_send()
    for o in range(1, rows):
        w1(o).wait_send()
        w3_wait(o)
    for i in range(rows):
        gweight_ref[pl.ds(i * piece, piece), :] = w_all[i].astype(F32) * scale
    for o in range(1, rows):
        w3(o).wait_send()


def shards(features, weight, out_bias, cotangent, adj_tiles, tile_cols, tile_counts):
    nd, width = features.shape
    tile = adj_tiles.shape[-1]
    slots = adj_tiles.shape[3]
    tile_rows = adj_tiles.shape[2]
    rows, cols = lax.axis_size("row"), lax.axis_size("col")
    per = nd // tile
    col_tiles = rows * per
    chips = rows // 2
    blocks = adj_tiles.reshape(tile_rows * slots, tile, tile)
    columns = tile_cols.reshape(tile_rows, slots)
    counts = tile_counts.reshape(tile_rows)
    k = lax.broadcasted_iota(jnp.int32, (tile_rows, slots, col_tiles), 1)
    j = lax.broadcasted_iota(jnp.int32, (tile_rows, slots, col_tiles), 2)
    t = lax.broadcasted_iota(jnp.int32, (tile_rows, slots, col_tiles), 0)
    found = (columns[:, :, None] == j) & (k < counts[:, None, None])
    slot = jnp.min(jnp.where(found, (t % per) * slots + k, per * slots), axis=1)
    big = tile_rows * col_tiles * tile * tile * 2 > 16 * 2**20
    buffers = 2 if big else min(4, cols)
    piece = width // rows
    dma = lambda n: pltpu.SemaphoreType.DMA((n,))
    vmem = pl.BlockSpec(memory_space=pltpu.VMEM)
    scale = (nd * rows * cols) ** (-0.5)
    act, gfeat, gweight, gbias = pl.pallas_call(
        functools.partial(kernel, rows, cols, nd, slots, tile, buffers, scale),
        out_shape=(
            jax.ShapeDtypeStruct((nd, width), BF),
            jax.ShapeDtypeStruct((nd, width), BF),
            jax.ShapeDtypeStruct((width, width), F32),
            jax.ShapeDtypeStruct((1, width), F32),
        ),
        in_specs=[pl.BlockSpec(memory_space=pltpu.SMEM)] + [vmem] * 4 + [pl.BlockSpec(memory_space=pl.ANY)],
        out_specs=(vmem,) * 4,
        scratch_shapes=[
            pltpu.VMEM((tile_rows * tile, col_tiles * tile), BF),
            pltpu.VMEM((rows * nd, width), BF),
            pltpu.VMEM((cols * nd, width), BF),
            pltpu.VMEM(((cols + 1) * nd, width), BF),
            pltpu.VMEM((nd, width), F32),
            pltpu.VMEM((cols * nd, width), BF),
            pltpu.VMEM((width, nd), BF),
            pltpu.VMEM((width, rows * nd), F32),
            pltpu.VMEM((rows, width, nd), BF),
            pltpu.VMEM((chips, width, nd), BF),
            pltpu.VMEM((chips, width, nd), BF),
            pltpu.VMEM((width, nd), BF),
            pltpu.VMEM((rows, piece + 16, width), BF),
            pltpu.VMEM((rows, piece + 16, width), BF),
            pltpu.VMEM((cols, piece, width), BF),
            pltpu.VMEM((rows, piece, width), BF),
            dma(buffers),
            dma(chips), dma(chips), dma(chips), dma(chips),
            dma(cols), dma(cols), dma(cols), dma(cols),
            dma(cols), dma(cols), dma(cols),
            dma(chips), dma(chips), dma(chips), dma(chips),
            dma(rows), dma(rows), dma(cols), dma(cols), dma(rows), dma(rows),
        ] + [pltpu.VMEM((per * slots + 1, tile, tile), BF)] * buffers,
        compiler_params=pltpu.CompilerParams(
            collective_id=0, has_side_effects=True, vmem_limit_bytes=(63 if big else 48) * 2**20
        ),
    )(slot, features, weight, out_bias.reshape(1, width), cotangent, blocks)
    return act, gfeat, gweight, gbias.reshape(width)


def solution(mesh):
    in_specs = (
        P(("row", "col"), None),
        P(),
        P(),
        P(("row", "col"), None),
        P("row", "col", None, None, None, None),
        P("row", "col", None, None),
        P("row", "col", None),
    )
    out_specs = (P(("row", "col"), None), P(("row", "col"), None), P(), P())
    return jax.shard_map(shards, mesh=mesh, in_specs=in_specs, out_specs=out_specs, check_vma=False)
```

```python
import functools

import jax
import jax.numpy as jnp
from jax import lax
from jax.experimental import pallas as pl
from jax.experimental.pallas import tpu as pltpu
from jax.sharding import PartitionSpec as P

MESH = pl.DeviceIdType.MESH
BF = jnp.bfloat16
F32 = jnp.float32


def aligned(index, size):
    return pl.ds(pl.multiple_of(index * size, size), size)


def kernel(
    rows, cols, nd, slots, tile, buffers, scale,
    slot_ref, feat_ref, weight_ref, bias_ref, cot_ref, adj_ref,
    act_ref, gfeat_ref, gweight_ref, gbias_ref,
    dense, panel, part, inbox, total, grads, grad_t, acc, back, sib_in, row_in,
    feat_t, w_out, w_in, w_col, w_all,
    load_sem, ag_send, ag_recv, fw_send, fw_recv, up_send, up_recv, dn_send, dn_recv,
    gu_send, gd_send, g_recv, sb_send, sb_recv, rs_send, rs_recv,
    w1_send, w1_recv, w2_send, w2_recv, w3_send, w3_recv,
    *tiles,
):
    r, z = lax.axis_index("row"), lax.axis_index("col")
    width = feat_ref.shape[1]
    chips = rows // 2
    chip, core = r // 2, r % 2
    sibling = 2 * chip + 1 - core
    per = nd // tile
    group = per * slots
    col_tiles = rows * per
    piece = width // rows

    def remote(src, dst, send, recv, row, col):
        return pltpu.make_async_remote_copy(
            src_ref=src, dst_ref=dst, send_sem=send, recv_sem=recv,
            device_id=(row, col), device_id_type=MESH,
        )

    def load(g):
        return pltpu.make_async_copy(
            adj_ref.at[pl.ds(g * group, group)],
            tiles[g % buffers].at[pl.ds(0, group)],
            load_sem.at[g % buffers],
        )

    for g in range(min(buffers, cols)):
        load(g).start()

    barrier = pltpu.get_barrier_semaphore()
    for o in range(1, rows):
        pl.semaphore_signal(barrier, inc=1, device_id=((r + o) % rows, z), device_id_type=MESH)
    for o in range(1, cols):
        pl.semaphore_signal(barrier, inc=1, device_id=(r, (z + o) % cols), device_id_type=MESH)
    projected = jnp.dot(feat_ref[...], weight_ref[...], preferred_element_type=F32).astype(BF)
    mine = aligned(r, nd)
    panel[mine, :] = projected
    pl.semaphore_wait(barrier, rows + cols - 2)

    def ag(o, to):
        return remote(panel.at[mine], panel.at[mine], ag_send.at[o], ag_recv.at[o], to, z)

    def forward(o):
        src = aligned(2 * ((chip + chips - o) % chips) + core, nd)
        return remote(panel.at[src], panel.at[src], fw_send.at[o], fw_recv.at[o], sibling, z)

    def forward_in(o):
        src = aligned(2 * ((chip + chips - o) % chips) + 1 - core, nd)
        return remote(panel.at[src], panel.at[src], fw_send.at[o], fw_recv.at[o], sibling, z)

    for o in range(1, chips):
        ag(o, 2 * ((chip + o) % chips) + core).start()
    forward(0).start()

    feat_t[...] = feat_ref[...].astype(F32).T.astype(BF)
    for b in range(buffers):
        tiles[b][group] = jnp.zeros((tile, tile), BF)
    for g in range(cols):
        buf = tiles[g % buffers]
        load(g).wait()

        def spread(t, carry, g=g, buf=buf):
            at = aligned(g * per + t, tile)
            for j in range(col_tiles):
                dense[at, pl.ds(j * tile, tile)] = buf[slot_ref[g * per + t, j]]
            return carry

        lax.fori_loop(0, per, spread, 0)
        if g + buffers < cols:
            load(g + buffers).start()

    for o in range(1, chips):
        src = aligned(2 * ((chip + chips - o) % chips) + core, nd)
        remote(panel.at[src], panel.at[src], ag_send.at[o], ag_recv.at[o], r, z).wait_recv()
        forward(o).start()
    for o in range(chips):
        forward_in(o).wait_recv()

    half = nd // 2

    def up_copy(d):
        return remote(part.at[aligned(d, half)], inbox.at[aligned(d + 2, half)], up_send.at[d], up_recv.at[d], r, z + 1)

    def up_wait(d):
        remote(part.at[aligned(d, half)], inbox.at[aligned(d + 2, half)], up_send.at[d], up_recv.at[d], r, z).wait_recv()

    def down_copy(d):
        return remote(part.at[aligned(d, half)], inbox.at[aligned(d, half)], dn_send.at[d], dn_recv.at[d], r, z - 1)

    def down_wait(d):
        remote(part.at[aligned(d, half)], inbox.at[aligned(d, half)], dn_send.at[d], dn_recv.at[d], r, z).wait_recv()

    low = (z < cols // 2).astype(jnp.int32)

    def produce(s, carry):
        d = low * (cols - 1 - s) + (1 - low) * s
        at = aligned(d, nd)
        part[at, :] = jnp.dot(dense[at, :], panel[...], preferred_element_type=F32).astype(BF)

        @pl.when((z == 0) & (d > z))
        def _():
            @pl.when(s > 0)
            def _():
                up_copy(2 * d + 3).wait_send()

            up_copy(2 * d).start()
            up_copy(2 * d).wait_send()
            up_copy(2 * d + 1).start()

        @pl.when((z == cols - 1) & (d < z))
        def _():
            @pl.when(s > 0)
            def _():
                down_copy(2 * d - 1).wait_send()

            down_copy(2 * d).start()
            down_copy(2 * d).wait_send()
            down_copy(2 * d + 1).start()

        return carry

    lax.fori_loop(0, cols, produce, 0)

    for s in range(cols):
        d = cols - 1 - s

        @pl.when((d > z) & (z > 0))
        def _(d=d):
            for u in (2 * d, 2 * d + 1):
                at = pl.ds(u * half, half)
                up_wait(u)
                part[at, :] = (part[at, :].astype(F32) + inbox[pl.ds((u + 2) * half, half), :].astype(F32)).astype(BF)
                up_copy(u).start()

        @pl.when((s < z) & (z < cols - 1))
        def _(d=s):
            for u in (2 * d, 2 * d + 1):
                at = pl.ds(u * half, half)
                down_wait(u)
                part[at, :] = (part[at, :].astype(F32) + inbox[at, :].astype(F32)).astype(BF)
                down_copy(u).start()

    here = aligned(z, nd)
    total[...] = part[here, :].astype(F32) + bias_ref[...]

    @pl.when(z > 0)
    def _():
        up_wait(2 * z)
        up_wait(2 * z + 1)
        total[...] += inbox[aligned(z + 1, nd), :].astype(F32)

    @pl.when(z < cols - 1)
    def _():
        down_wait(2 * z)
        down_wait(2 * z + 1)
        total[...] += inbox[here, :].astype(F32)

    preact = total[...]
    sig = jax.nn.sigmoid(preact)
    grads[here, :] = (cot_ref[...].astype(F32) * sig * (1.0 + preact * (1.0 - sig))).astype(BF)

    def g_copy(b, send, to):
        return remote(grads.at[aligned(b, nd)], grads.at[aligned(b, nd)], send.at[b], g_recv.at[b], r, to)

    @pl.when(z < cols - 1)
    def _():
        g_copy(z, gu_send, z + 1).start()

    @pl.when(z > 0)
    def _():
        g_copy(z, gd_send, z - 1).start()

    act_ref[...] = (preact * sig).astype(BF)

    span = 2 * nd

    def backward(b, first):
        grad_t[...] = grads[aligned(b, nd), :].astype(F32).T.astype(BF)
        at = aligned(b, nd)

        def step(i, carry):
            lanes = aligned(i, span)
            product = jnp.dot(grad_t[...], dense[at, lanes], preferred_element_type=F32)
            if first:
                acc[:, lanes] = product
            else:
                acc[:, lanes] += product
            return carry

        lax.fori_loop(0, rows // 2, step, 0)

    backward(z, True)
    for o in range(1, cols):

        @pl.when(z - o >= 0)
        def _(o=o):
            g_copy(z - o, gu_send, z).wait_recv()

            @pl.when(z < cols - 1)
            def _():
                g_copy(z - o, gu_send, z + 1).start()

        @pl.when(z + o < cols)
        def _(o=o):
            g_copy(z + o, gd_send, z).wait_recv()

            @pl.when(z > 0)
            def _():
                g_copy(z + o, gd_send, z - 1).start()

        @pl.when(z - o >= 0)
        def _(o=o):
            backward(z - o, False)

        @pl.when(z + o < cols)
        def _(o=o):
            backward(z + o, False)

    def sib_copy(m):
        return remote(back.at[2 * m + 1 - core], sib_in.at[m], sb_send.at[m], sb_recv.at[m], sibling, z)

    def lanes_of(dest):
        return aligned(dest, nd)

    for o in range(chips):
        m = (chip + 1 + o) % chips
        dest = 2 * m + 1 - core
        back[dest] = acc[:, lanes_of(dest)].astype(BF)
        sib_copy(m).start()

    def row_copy(o):
        m = (chip + o) % chips
        return remote(back.at[2 * m + core], row_in.at[o], rs_send.at[o], rs_recv.at[o], 2 * m + core, z)

    for o in range(1, chips):
        m = (chip + o) % chips
        dest = 2 * m + core
        sib_copy(m).wait_recv()
        back[dest] = (acc[:, lanes_of(dest)] + sib_in[m].astype(F32)).astype(BF)
        row_copy(o).start()

    bias_row = jnp.sum(grads[...].astype(F32), axis=0, keepdims=True)
    high = bias_row.astype(BF)
    rest = (bias_row - high.astype(F32)).astype(BF).astype(F32)
    line = lax.broadcasted_iota(jnp.int32, (16, width), 0)
    bias_rows = jnp.where(line == 0, high.astype(F32), jnp.where(line == 1, rest, 0.0)).astype(BF)

    sib_copy(chip).wait_recv()
    summed = acc[:, lanes_of(r)] + sib_in[chip].astype(F32)
    for o in range(1, chips):
        row_copy(o).wait_recv()
        summed = summed + row_in[o].astype(F32)
    gp = summed.T.astype(BF)

    w_part = jnp.dot(feat_t[...], gp, preferred_element_type=F32).astype(BF)
    for i in range(rows):
        w_out[i, pl.ds(0, piece), :] = w_part[i * piece:(i + 1) * piece]
        w_out[i, pl.ds(piece, 16), :] = bias_rows

    def w1(o):
        to = (r + o) % rows
        return remote(w_out.at[to], w_in.at[r], w1_send.at[o], w1_recv.at[o], to, z)

    def w1_wait(o):
        src = (r + rows - o) % rows
        remote(w_out.at[src], w_in.at[src], w1_send.at[o], w1_recv.at[o], src, z).wait_recv()

    for o in range(1, rows):
        w1(o).start()
    w_in[r] = w_out[r]
    gfeat_ref[...] = lax.dot_general(
        gp, weight_ref[...], (((1,), (1,)), ((), ())), preferred_element_type=F32
    ).astype(BF)
    for o in range(1, rows):
        w1_wait(o)
    part_sum = w_in[0].astype(F32)
    for i in range(1, rows):
        part_sum = part_sum + w_in[i].astype(F32)
    w_col[z] = part_sum[:piece].astype(BF)

    def w2(o):
        to = (z + o) % cols
        return remote(w_col.at[z], w_col.at[z], w2_send.at[o], w2_recv.at[o], r, to)

    def w2_wait(o):
        src = (z + cols - o) % cols
        remote(w_col.at[src], w_col.at[src], w2_send.at[o], w2_recv.at[o], r, src).wait_recv()

    for o in range(1, cols):
        w2(o).start()
    gbias_ref[...] = (part_sum[piece:piece + 1] + part_sum[piece + 1:piece + 2]) * scale
    for o in range(1, cols):
        w2_wait(o)
    col_sum = w_col[0].astype(F32)
    for i in range(1, cols):
        col_sum = col_sum + w_col[i].astype(F32)
    w_all[r] = col_sum.astype(BF)

    def w3(o):
        to = (r + o) % rows
        return remote(w_all.at[r], w_all.at[r], w3_send.at[o], w3_recv.at[o], to, z)

    def w3_wait(o):
        src = (r + rows - o) % rows
        remote(w_all.at[src], w_all.at[src], w3_send.at[o], w3_recv.at[o], src, z).wait_recv()

    for o in range(1, rows):
        w3(o).start()

    for o in range(1, chips):
        ag(o, 2 * ((chip + o) % chips) + core).wait_send()
        row_copy(o).wait_send()
    for o in range(chips):
        forward(o).wait_send()
        sib_copy((chip + 1 + o) % chips).wait_send()
    for d in range(cols):

        @pl.when((d > z) & (z > 0))
        def _(d=d):
            up_copy(2 * d).wait_send()

        @pl.when((d > z) & ((z > 0) | (d == z + 1)))
        def _(d=d):
            up_copy(2 * d + 1).wait_send()

        @pl.when((d < z) & (z < cols - 1))
        def _(d=d):
            down_copy(2 * d).wait_send()

        @pl.when((d < z) & ((z < cols - 1) | (d == z - 1)))
        def _(d=d):
            down_copy(2 * d + 1).wait_send()

        @pl.when((d <= z) & (z < cols - 1))
        def _(d=d):
            g_copy(d, gu_send, z + 1).wait_send()

        @pl.when((d >= z) & (z > 0))
        def _(d=d):
            g_copy(d, gd_send, z - 1).wait_send()

    for o in range(1, cols):
        w2(o).wait_send()
    for o in range(1, rows):
        w1(o).wait_send()
        w3_wait(o)
    for i in range(rows):
        gweight_ref[pl.ds(i * piece, piece), :] = w_all[i].astype(F32) * scale
    for o in range(1, rows):
        w3(o).wait_send()


def shards(features, weight, out_bias, cotangent, adj_tiles, tile_cols, tile_counts):
    nd, width = features.shape
    tile = adj_tiles.shape[-1]
    slots = adj_tiles.shape[3]
    tile_rows = adj_tiles.shape[2]
    rows, cols = lax.axis_size("row"), lax.axis_size("col")
    per = nd // tile
    col_tiles = rows * per
    chips = rows // 2
    blocks = adj_tiles.reshape(tile_rows * slots, tile, tile)
    columns = tile_cols.reshape(tile_rows, slots)
    counts = tile_counts.reshape(tile_rows)
    k = lax.broadcasted_iota(jnp.int32, (tile_rows, slots, col_tiles), 1)
    j = lax.broadcasted_iota(jnp.int32, (tile_rows, slots, col_tiles), 2)
    t = lax.broadcasted_iota(jnp.int32, (tile_rows, slots, col_tiles), 0)
    found = (columns[:, :, None] == j) & (k < counts[:, None, None])
    slot = jnp.min(jnp.where(found, (t % per) * slots + k, per * slots), axis=1)
    big = tile_rows * col_tiles * tile * tile * 2 > 16 * 2**20
    buffers = 2 if big else min(4, cols)
    piece = width // rows
    dma = lambda n: pltpu.SemaphoreType.DMA((n,))
    vmem = pl.BlockSpec(memory_space=pltpu.VMEM)
    scale = (nd * rows * cols) ** (-0.5)
    act, gfeat, gweight, gbias = pl.pallas_call(
        functools.partial(kernel, rows, cols, nd, slots, tile, buffers, scale),
        out_shape=(
            jax.ShapeDtypeStruct((nd, width), BF),
            jax.ShapeDtypeStruct((nd, width), BF),
            jax.ShapeDtypeStruct((width, width), F32),
            jax.ShapeDtypeStruct((1, width), F32),
        ),
        in_specs=[pl.BlockSpec(memory_space=pltpu.SMEM)] + [vmem] * 4 + [pl.BlockSpec(memory_space=pl.ANY)],
        out_specs=(vmem,) * 4,
        scratch_shapes=[
            pltpu.VMEM((tile_rows * tile, col_tiles * tile), BF),
            pltpu.VMEM((rows * nd, width), BF),
            pltpu.VMEM((cols * nd, width), BF),
            pltpu.VMEM(((cols + 1) * nd, width), BF),
            pltpu.VMEM((nd, width), F32),
            pltpu.VMEM((cols * nd, width), BF),
            pltpu.VMEM((width, nd), BF),
            pltpu.VMEM((width, rows * nd), F32),
            pltpu.VMEM((rows, width, nd), BF),
            pltpu.VMEM((chips, width, nd), BF),
            pltpu.VMEM((chips, width, nd), BF),
            pltpu.VMEM((width, nd), BF),
            pltpu.VMEM((rows, piece + 16, width), BF),
            pltpu.VMEM((rows, piece + 16, width), BF),
            pltpu.VMEM((cols, piece, width), BF),
            pltpu.VMEM((rows, piece, width), BF),
            dma(buffers),
            dma(chips), dma(chips), dma(chips), dma(chips),
            dma(2 * cols), dma(2 * cols), dma(2 * cols), dma(2 * cols),
            dma(cols), dma(cols), dma(cols),
            dma(chips), dma(chips), dma(chips), dma(chips),
            dma(rows), dma(rows), dma(cols), dma(cols), dma(rows), dma(rows),
        ] + [pltpu.VMEM((per * slots + 1, tile, tile), BF)] * buffers,
        compiler_params=pltpu.CompilerParams(
            collective_id=0, has_side_effects=True, vmem_limit_bytes=(63 if big else 48) * 2**20
        ),
    )(slot, features, weight, out_bias.reshape(1, width), cotangent, blocks)
    return act, gfeat, gweight, gbias.reshape(width)


def solution(mesh):
    in_specs = (
        P(("row", "col"), None),
        P(),
        P(),
        P(("row", "col"), None),
        P("row", "col", None, None, None, None),
        P("row", "col", None, None),
        P("row", "col", None),
    )
    out_specs = (P(("row", "col"), None), P(("row", "col"), None), P(), P())
    return jax.shard_map(shards, mesh=mesh, in_specs=in_specs, out_specs=out_specs, check_vma=False)
```
